512 devices in a mesh: users: 128 (over z, y, core), heads: 4 (over x).
Axes of the slice: x: 4, y: 8, z: 8, core: 2. Of those that a mesh axis runs over, the one named last changes fastest.
Arguments:
- history: bfloat16 [128, 4096, 512], P('users'), may hold values from -6 to 6
- candidates: bfloat16 [128, 1024, 512], P('users'), may hold values from -70 to 70
- lengths: int32 [128], replicated, may hold values from 512 to 4096, as said below
- counts: int32 [128], replicated, may hold values from 128 to 1024, as said below
- w_query: bfloat16 [512, 512], P(None, 'heads'), may hold values from -0.25 to 0.25
- w_key: bfloat16 [512, 512], P(None, 'heads'), may hold values from -0.25 to 0.25
- w_value: bfloat16 [512, 512], P(None, 'heads'), may hold values from -0.25 to 0.25
- w_out: bfloat16 [512, 512], P('heads'), may hold values from -0.375 to 0.375
Outputs:
- mixed: float32 [128, 1024, 512], P('users', None, 'heads')
The draws below stay inside these ranges and needn't reach their ends.
Inputs may be any that keep to these rules, and one draw needn't show every extreme that they name: `lengths`: one user has exactly 4096 events. `counts`: one user has exactly 1024 candidates.
All inputs are finite; a program needn't handle non-finite values.
Results may differ from the reference program's by a relative error of at most 0.0085.
The reference program's roundings to bfloat16 on the way (of `query`, `weight` and `attended`) count: a program that leaves them out, or rounds other values in their place, can miss the bound.
Values may be sent and summed in bfloat16 or wider, within the bound.
A program may use at most 128 MiB of HBM per device.

```python
import jax
import jax.numpy as jnp
from jax import lax

D = 512
H = 8
HD = 64
CH = 256
LMAX = 4096
CMAX = 1024
USERS = 128


def draw_candidates(key, part):
    key = jax.random.fold_in(key, 7)
    first = jax.random.fold_in(key, 0)
    values = jnp.clip(jax.random.normal(first, (USERS, CMAX, D), jnp.float32), -6.0, 6.0)
    return values.astype(jnp.bfloat16)


def draw_lengths(key, part):
    key = jax.random.fold_in(key, 11)
    first, second, third = jax.random.split(key, 3)
    shift = jax.random.randint(first, (USERS,), 0, 5)
    base = jnp.right_shift(jnp.full((USERS,), LMAX, jnp.int32), shift)
    cut = jax.random.randint(second, (USERS,), 0, base // 2 + 1)
    chosen = jax.random.randint(third, (), 0, USERS)
    result = jnp.maximum(base - cut, 2 * CH)
    return jnp.where(jnp.arange(USERS) == chosen, LMAX, result).astype(jnp.int32)


def draw_counts(key, part):
    key = jax.random.fold_in(key, 13)
    first, second = jax.random.split(key)
    result = jax.random.randint(first, (USERS,), CMAX // 8, CMAX + 1)
    chosen = jax.random.randint(second, (), 0, USERS)
    return jnp.where(jnp.arange(USERS) == chosen, CMAX, result).astype(jnp.int32)


def spiked(entries, stream_key, source, target, parts, factor):
    owner, partner = [(jnp.arange(entries.shape[position]) // (entries.shape[position] // parts)).reshape([-1 if axis == position else 1 for axis in range(entries.ndim)]) for position in (source, target)]
    chosen = jax.random.permutation(stream_key, parts)[partner]
    strong = (owner == chosen) | (owner == (partner + parts // 2) % parts)
    return jnp.where(strong, factor * entries, entries)


def levels(own_key, dims, shards, least, top_value):
    def one(position, blocks):
        draws = jax.random.uniform(jax.random.fold_in(jax.random.fold_in(own_key, 6), position), (blocks,), jnp.float32, least / len(shards), top_value / len(shards))
        return jnp.repeat(jnp.exp(draws), dims[position] // blocks).reshape((-1,) + (1,) * (len(dims) - position - 1))

    factor_of = one(*shards[0])
    for cut in shards[1:]:
        factor_of = factor_of * one(*cut)
    return factor_of


def scatter_about(rng, shape, spread, most, pieces=(), held_as=jnp.bfloat16):
    factor_of = levels(rng, shape, pieces, -0.22, 0.18) if pieces else 1.0
    values = jax.random.normal(rng, shape, jnp.float32) * spread * factor_of
    return jnp.minimum(jnp.maximum(values, -most), most).astype(held_as)


def heavy_noise(stream_key, shape, width, bound, shards, heavy, held_as=jnp.bfloat16):
    array = width * jax.random.normal(stream_key, shape, jnp.float32)
    if shards:
        array = array * levels(stream_key, shape, shards, -0.22, 0.18)
    return jnp.clip(spiked(array, jax.random.fold_in(stream_key, 3), *heavy), -bound, bound).astype(held_as)


def setup_inputs(seed: int = 0) -> dict:
    arg_keys = jax.random.split(jax.random.key(seed), 9)
    return {
        "history": scatter_about(arg_keys[0], (USERS, LMAX, D), 1.0, 6.0, ((0, 128),)),
        "candidates": draw_candidates(jax.random.fold_in(arg_keys[8], 71), 0),
        "lengths": draw_lengths(jax.random.fold_in(arg_keys[8], 71), 0),
        "counts": draw_counts(jax.random.fold_in(arg_keys[8], 71), 0),
        "w_query": scatter_about(arg_keys[4], (D, H * HD), D ** -0.5, 0.25, ((1, 4),)),
        "w_key": scatter_about(arg_keys[5], (D, H * HD), D ** -0.5, 0.25, ((1, 4),)),
        "w_value": scatter_about(arg_keys[6], (D, H * HD), D ** -0.5, 0.25, ((1, 4),)),
        "w_out": heavy_noise(arg_keys[7], (H * HD, D), (H * HD) ** -0.5, 0.375, ((0, 4),), (0, 1, 4, 2.0)),
    }


def one_user(items, w_query, w_key, w_value, w_out):
    hist, cand, length, count = items
    scale = HD ** -0.5
    query = (jnp.dot(cand, w_query, preferred_element_type=jnp.float32) * scale).astype(jnp.bfloat16)
    query = query.reshape(CMAX, H, HD).astype(jnp.float32)
    key = jnp.dot(hist, w_key, preferred_element_type=jnp.float32).astype(jnp.bfloat16)
    value = jnp.dot(hist, w_value, preferred_element_type=jnp.float32).astype(jnp.bfloat16)
    key = key.reshape(LMAX, H, HD).astype(jnp.float32)
    value = value.reshape(LMAX, H, HD).astype(jnp.float32)
    score = jnp.einsum("chd,khd->hck", query, key)
    valid = jnp.arange(LMAX, dtype=jnp.int32) < length
    score = jnp.where(valid[None, None, :], score, -jnp.inf)
    top = jnp.max(score, axis=-1, keepdims=True)
    weight = jnp.exp(score - top)
    total = jnp.sum(weight, axis=-1)
    weight = weight.astype(jnp.bfloat16).astype(jnp.float32)
    attended = (jnp.einsum("hck,khd->hcd", weight, value) / total[..., None]).astype(jnp.bfloat16)
    attended = attended.astype(jnp.float32)
    rows = w_out.astype(jnp.float32).reshape(H, HD, D)
    summed = jnp.einsum("hcd,hde->ce", attended, rows)
    live = jnp.arange(CMAX, dtype=jnp.int32) < count
    return jnp.where(live[:, None], summed, jnp.float32(0.0))


def reference(history, candidates, lengths, counts, w_query, w_key, w_value, w_out):
    def apply(items):
        return one_user(items, w_query, w_key, w_value, w_out)
    return lax.map(apply, (history, candidates, lengths, counts))
```

```python
import jax
import jax.numpy as jnp
from jax import lax
from jax.experimental import pallas as pl
from jax.experimental.pallas import tpu as pltpu
from jax.sharding import PartitionSpec as P

D = 512
HD = 64
LMAX = 4096
CMAX = 1024
GROUP = 128
TILE = 128
STEPS = CMAX // TILE
WIDE = 2 * TILE
SPAN = 2048
LOAD = 512
LOADS = LMAX // LOAD
VROWS = GROUP + 16
FOLD = 64
MESH = pl.DeviceIdType.MESH
BF = jnp.bfloat16
F32 = jnp.float32


def kernel(
    history, candidates, lengths, counts, w_query, w_key, w_value, w_out, out,
    hist, cand, wq, wkv, wo, wo_all, keys, values, query, score0, score1, top, att, done,
    load_sem, wo_send, wo_recv, send_sem, recv_sem, out_sem,
):
    user = lax.axis_index("users")
    me = lax.axis_index("heads")
    ring = lax.axis_size("heads")
    right = lax.rem(me + 1, ring)
    left = lax.rem(me + ring - 1, ring)
    across = lax.rem(me + 2, ring)

    def load(source, target, slot):
        copy = pltpu.make_async_copy(source, target, load_sem.at[slot])
        copy.start()
        return copy

    wq_copy = load(w_query, wq, 0)
    first_cand = load(candidates.at[0, pl.ds(0, WIDE)], cand.at[pl.ds(0, WIDE)], 1)
    wk_copy = load(w_key, wkv.at[:, pl.ds(0, GROUP)], 2)
    wv_copy = load(w_value, wkv.at[:, pl.ds(GROUP, GROUP)], 3)
    hist_copies = [
        load(history.at[0, pl.ds(i * LOAD, LOAD)], hist.at[pl.ds(i * LOAD, LOAD)], 6 + i)
        for i in range(LOADS)
    ]
    rest_cand = load(
        candidates.at[0, pl.ds(WIDE, CMAX - WIDE)], cand.at[pl.ds(WIDE, CMAX - WIDE)], 4
    )
    wo_copy = load(w_out, wo, 5)

    barrier = pltpu.get_barrier_semaphore()
    for peer in (left, right, across):
        pl.semaphore_signal(barrier, inc=1, device_id={"heads": peer}, device_id_type=MESH)

    length = lengths[user]
    count = counts[user]

    def make_query(step, slot):
        rows = cand[pl.ds(pl.multiple_of(step * TILE, TILE), TILE), :]
        q = (jnp.dot(rows, wq[...], preferred_element_type=F32) * HD ** (-0.5)).astype(BF)
        first = lax.broadcasted_iota(jnp.int32, (TILE, GROUP), 1) < HD
        query[slot, :TILE] = jnp.where(first, q, jnp.zeros_like(q))
        query[slot, TILE:] = jnp.where(first, jnp.zeros_like(q), q)

    def scores(q, target, start, rows, best):
        s = lax.dot_general(
            keys[start : start + rows, :], q, (((1,), (1,)), ((), ())), preferred_element_type=F32
        )
        target[start : start + rows, :] = s
        s = jnp.max(s.reshape(rows // FOLD, FOLD, WIDE), axis=0)
        return s if best is None else jnp.maximum(best, s)

    def weigh(source, start, shift, total):
        p = jnp.exp(source[start : start + SPAN, :] - shift).astype(BF)
        r = jnp.dot(values[:, start : start + SPAN], p, preferred_element_type=F32)
        return r if total is None else total + r

    def keep_top(best):
        top[...] = jnp.broadcast_to(jnp.max(best, axis=0, keepdims=True), (8, WIDE))

    wq_copy.wait()
    first_cand.wait()
    make_query(0, 0)
    make_query(1, 1)
    wk_copy.wait()
    wv_copy.wait()
    q = query[0]
    best = None
    key0 = None
    for i in range(LOADS):
        start = i * LOAD
        hist_copies[i].wait()
        kv = jnp.dot(hist[start : start + LOAD, :], wkv[...], preferred_element_type=F32)
        place = start + lax.broadcasted_iota(jnp.int32, (LOAD, GROUP), 0)
        valid = place < length
        k = kv[:, :GROUP]
        if i == 0:
            key0 = k[0:1, :]
        else:
            k = jnp.where(valid, k, key0)
        keys[start : start + LOAD, :] = k.astype(BF)
        v = jnp.where(valid, kv[:, GROUP:], 0.0)
        values[0:GROUP, start : start + LOAD] = v.T.astype(BF)
        row = lax.broadcasted_iota(jnp.int32, (VROWS - GROUP, LOAD), 0)
        place = start + lax.broadcasted_iota(jnp.int32, (VROWS - GROUP, LOAD), 1)
        ones = jnp.where((row == 0) & (place < length), 1.0, 0.0)
        values[GROUP:, start : start + LOAD] = ones.astype(BF)
        best = scores(q, score0, start, LOAD, best)
    keep_top(best)
    rest_cand.wait()
    wo_copy.wait()

    pl.semaphore_wait(barrier, 3)

    def block(peer):
        return wo.at[:, pl.ds(pl.multiple_of(peer * GROUP, GROUP), GROUP)]

    wo_sends = []
    for slot, peer in ((1, right), (2, left), (3, across)):
        copy = pltpu.make_async_remote_copy(
            src_ref=block(peer), dst_ref=wo_all.at[slot], send_sem=wo_send.at[slot],
            recv_sem=wo_recv.at[slot], device_id={"heads": peer}, device_id_type=MESH,
        )
        copy.start()
        wo_sends.append(copy)
    wo_own = pltpu.make_async_copy(block(me), wo_all.at[0], wo_send.at[0])
    wo_own.start()

    HALF = TILE // 2

    def to_right(step):
        return pltpu.make_async_remote_copy(
            src_ref=att.at[0, step], dst_ref=att.at[1, step], send_sem=send_sem.at[0, step],
            recv_sem=recv_sem.at[0, step], device_id={"heads": right}, device_id_type=MESH,
        )

    def to_left(step):
        return pltpu.make_async_remote_copy(
            src_ref=att.at[0, step], dst_ref=att.at[2, step], send_sem=send_sem.at[1, step],
            recv_sem=recv_sem.at[1, step], device_id={"heads": left}, device_id_type=MESH,
        )

    def on_right(step):
        return pltpu.make_async_remote_copy(
            src_ref=att.at[1, step, pl.ds(0, HALF)], dst_ref=att.at[3, step, pl.ds(0, HALF)],
            send_sem=send_sem.at[2, step], recv_sem=recv_sem.at[2, step],
            device_id={"heads": right}, device_id_type=MESH,
        )

    def on_left(step):
        return pltpu.make_async_remote_copy(
            src_ref=att.at[2, step, pl.ds(HALF, HALF)], dst_ref=att.at[3, step, pl.ds(HALF, HALF)],
            send_sem=send_sem.at[3, step], recv_sem=recv_sem.at[3, step],
            device_id={"heads": left}, device_id_type=MESH,
        )

    def finish(step, total):
        ones = total[GROUP : GROUP + 1]
        first = total[:HD, :TILE] / ones[:, :TILE]
        second = total[HD:GROUP, TILE:] / ones[:, TILE:]
        att[0, step] = jnp.concatenate([first, second], axis=0).T.astype(BF)

    def send(step):
        to_right(step).start()
        to_left(step).start()

    def forward(step):
        to_right(step).wait_recv()
        to_left(step).wait_recv()
        on_right(step).start()
        on_left(step).start()

    def arrived(step):
        on_right(step).wait_recv()
        on_left(step).wait_recv()

    def out_copy(step):
        return pltpu.make_async_copy(
            done.at[step], out.at[0, pl.ds(pl.multiple_of(step * TILE, TILE), TILE)], out_sem.at[step]
        )

    def project(step):
        r = jnp.dot(att[0, step], wo_all[0], preferred_element_type=F32)
        for slot in (1, 2, 3):
            r += jnp.dot(att[slot, step], wo_all[slot], preferred_element_type=F32)
        row = step * TILE + lax.broadcasted_iota(jnp.int32, (TILE, GROUP), 0)
        done[step] = jnp.where(row < count, r, 0.0)

    def tile(step, source, target, slot):
        shift = top[0:1, :]
        total = None
        best = None
        if target is not None:
            q = query[1 - slot]
        for start in range(0, LMAX, SPAN):
            if target is not None:
                best = scores(q, target, start, SPAN, best)
            total = weigh(source, start, shift, total)
        if target is not None:
            keep_top(best)
        finish(step, total)

    def exchange(step, peeled):
        send(step)

        def forward_last():
            forward(step - 1)

        def project_last():
            arrived(step - 2)
            project(step - 2)
            out_copy(step - 2).start()

        if peeled:
            forward_last()
            project_last()
        else:
            pl.when(step >= 1)(forward_last)
            pl.when(step >= 2)(project_last)

    for copy in wo_sends:
        copy.wait_recv()
    wo_own.wait()

    @pl.loop(0, STEPS // 2 - 1)
    def _(pair):
        step = 2 * pair
        tile(step, score0, score1, 0)
        make_query(step + 2, 0)
        exchange(step, False)
        tile(step + 1, score1, score0, 1)
        make_query(step + 3, 1)
        exchange(step + 1, False)

    tile(STEPS - 2, score0, score1, 0)
    exchange(STEPS - 2, True)
    tile(STEPS - 1, score1, None, 1)
    exchange(STEPS - 1, True)
    forward(STEPS - 1)
    for step in (STEPS - 2, STEPS - 1):
        arrived(step)
        project(step)
        out_copy(step).start()
    for copy in wo_sends:
        copy.wait_send()

    @pl.loop(0, STEPS)
    def _(step):
        to_right(step).wait_send()
        to_left(step).wait_send()
        on_right(step).wait_send()
        on_left(step).wait_send()
        out_copy(step).wait()


def body(history, candidates, lengths, counts, w_query, w_key, w_value, w_out):
    anywhere = pl.BlockSpec(memory_space=pl.ANY)
    scalar = pl.BlockSpec(memory_space=pltpu.SMEM)
    groups = lax.axis_size("heads")
    return pl.pallas_call(
        kernel,
        out_shape=jax.ShapeDtypeStruct((1, CMAX, GROUP), F32),
        in_specs=[anywhere, anywhere, scalar, scalar, anywhere, anywhere, anywhere, anywhere],
        out_specs=anywhere,
        scratch_shapes=[
            pltpu.VMEM((LMAX, D), BF),
            pltpu.VMEM((CMAX, D), BF),
            pltpu.VMEM((D, GROUP), BF),
            pltpu.VMEM((D, 2 * GROUP), BF),
            pltpu.VMEM((GROUP, D), BF),
            pltpu.VMEM((groups, GROUP, GROUP), BF),
            pltpu.VMEM((LMAX, GROUP), BF),
            pltpu.VMEM((VROWS, LMAX), BF),
            pltpu.VMEM((2, WIDE, GROUP), BF),
            pltpu.VMEM((LMAX, WIDE), F32),
            pltpu.VMEM((LMAX, WIDE), F32),
            pltpu.VMEM((8, WIDE), F32),
            pltpu.VMEM((groups, STEPS, TILE, GROUP), BF),
            pltpu.VMEM((STEPS, TILE, GROUP), F32),
            pltpu.SemaphoreType.DMA((6 + LOADS,)),
            pltpu.SemaphoreType.DMA((groups,)),
            pltpu.SemaphoreType.DMA((groups,)),
            pltpu.SemaphoreType.DMA((4, STEPS)),
            pltpu.SemaphoreType.DMA((4, STEPS)),
            pltpu.SemaphoreType.DMA((STEPS,)),
        ],
        compiler_params=pltpu.CompilerParams(
            collective_id=0, has_side_effects=True, vmem_limit_bytes=60 * 2**20
        ),
    )(history, candidates, lengths, counts, w_query, w_key, w_value, w_out)


def solution(mesh):
    placed = (
        P("users", None, None),
        P("users", None, None),
        P(),
        P(),
        P(None, "heads"),
        P(None, "heads"),
        P(None, "heads"),
        P("heads", None),
    )
    return jax.shard_map(
        body, mesh=mesh, in_specs=placed, out_specs=P("users", None, "heads"), check_vma=False
    )
```

```python
import jax
import jax.numpy as jnp
from jax import lax
from jax.experimental import pallas as pl
from jax.experimental.pallas import tpu as pltpu
from jax.sharding import PartitionSpec as P

D = 512
HD = 64
LMAX = 4096
CMAX = 1024
GROUP = 128
TILE = 128
STEPS = CMAX // TILE
WIDE = 2 * TILE
SPAN = 512
LOADS = (512, 1024, 1024, 1024, 512)
STARTS = tuple(sum(LOADS[:i]) for i in range(len(LOADS)))
VROWS = GROUP + 16
FOLD = 64
WO_AT = 3
MESH = pl.DeviceIdType.MESH
BF = jnp.bfloat16
F32 = jnp.float32


def kernel(
    history, candidates, lengths, counts, w_query, w_key, w_value, w_out, out,
    hist, cand, wq, wkv, wo, wo_all, keys, values, score, top, att,
    length_of, count_of, load_sem, wo_send, wo_recv, send_sem, recv_sem,
):
    user = lax.axis_index("users")
    me = lax.axis_index("heads")
    ring = lax.axis_size("heads")
    right = lax.rem(me + 1, ring)
    left = lax.rem(me + ring - 1, ring)
    across = lax.rem(me + 2, ring)

    def load(source, target, slot):
        copy = pltpu.make_async_copy(source, target, load_sem.at[slot])
        copy.start()
        return copy

    def load_history(i):
        rows = pl.ds(STARTS[i], LOADS[i])
        return load(history.at[0, rows], hist.at[rows], 8 + i)

    wk_copy = load(w_key, wkv.at[:, pl.ds(0, GROUP)], 2)
    wv_copy = load(w_value, wkv.at[:, pl.ds(GROUP, GROUP)], 3)
    hist_copies = [load_history(0)]
    length_copy = load(lengths, length_of, 6)
    wq_copy = load(w_query, wq, 0)
    first_cand = load(candidates.at[0, pl.ds(0, TILE)], cand.at[pl.ds(0, TILE)], 1)
    wo_copy = load(w_out, wo, 5)
    hist_copies += [load_history(i) for i in range(1, len(LOADS))]
    count_copy = load(counts, count_of, 7)
    rest_cand = load(
        candidates.at[0, pl.ds(TILE, CMAX - TILE)], cand.at[pl.ds(TILE, CMAX - TILE)], 4
    )

    barrier = pltpu.get_barrier_semaphore()
    for peer in (left, right, across):
        pl.semaphore_signal(barrier, inc=1, device_id={"heads": peer}, device_id_type=MESH)

    def make_query(step):
        rows = cand[pl.ds(pl.multiple_of(step * TILE, TILE), TILE), :]
        q = (jnp.dot(rows, wq[...], preferred_element_type=F32) * HD ** (-0.5)).astype(BF)
        first = lax.broadcasted_iota(jnp.int32, (TILE, GROUP), 1) < HD
        zero = jnp.zeros_like(q)
        return jnp.concatenate([jnp.where(first, q, zero), jnp.where(first, zero, q)], axis=0)

    def scores(k, q, place):
        s = lax.dot_general(k, q, (((1,), (1,)), ((), ())), preferred_element_type=F32)
        score[place, :] = s
        return jnp.max(s.reshape(-1, FOLD, WIDE), axis=0)

    def keep_top(highest):
        top[...] = jnp.broadcast_to(jnp.max(highest, axis=0, keepdims=True), (8, WIDE))

    def block(peer):
        return wo.at[:, pl.ds(pl.multiple_of(peer * GROUP, GROUP), GROUP)]

    wo_own = pltpu.make_async_copy(block(me), wo_all.at[0], wo_send.at[0])
    wo_sends = [
        pltpu.make_async_remote_copy(
            src_ref=block(peer), dst_ref=wo_all.at[slot], send_sem=wo_send.at[slot],
            recv_sem=wo_recv.at[slot], device_id={"heads": peer}, device_id_type=MESH,
        )
        for slot, peer in ((3, across), (1, right), (2, left))
    ]

    def exchange_wo():
        wo_copy.wait()
        pl.semaphore_wait(barrier, 3)
        for copy in wo_sends + [wo_own]:
            copy.start()

    wk_copy.wait()
    wv_copy.wait()
    length_copy.wait()
    length = length_of[user]
    highest = None
    for i, (start, size) in enumerate(zip(STARTS, LOADS)):
        place = pl.ds(start, size)
        hist_copies[i].wait()
        kv = jnp.dot(hist[place, :], wkv[...], preferred_element_type=F32)
        valid = start + lax.broadcasted_iota(jnp.int32, (size, GROUP), 0) < length
        if i == 0:
            key0 = kv[0:1, :GROUP]
        keys[place, :] = jnp.where(valid, kv[:, :GROUP], key0).astype(BF)
        values[0:GROUP, place] = jnp.where(valid, kv[:, GROUP:], 0.0).T.astype(BF)
        row = lax.broadcasted_iota(jnp.int32, (VROWS - GROUP, size), 0)
        column = start + lax.broadcasted_iota(jnp.int32, (VROWS - GROUP, size), 1)
        ones = jnp.where((row == 0) & (column < length), 1.0, 0.0)
        values[GROUP:, place] = ones.astype(BF)
        if i == 0:
            wq_copy.wait()
            first_cand.wait()
            q = make_query(0)
        else:
            before = pl.ds(STARTS[i - 1], LOADS[i - 1])
            s = scores(keys[before, :], q, before)
            highest = s if highest is None else jnp.maximum(highest, s)
        if i == WO_AT:
            exchange_wo()
    place = pl.ds(STARTS[-1], LOADS[-1])
    keep_top(jnp.maximum(highest, scores(keys[place, :], q, place)))
    rest_cand.wait()
    count_copy.wait()
    count = count_of[user]

    def sends(step):
        return [
            pltpu.make_async_remote_copy(
                src_ref=att.at[0, step], dst_ref=att.at[slot, step],
                send_sem=send_sem.at[slot, step], recv_sem=recv_sem.at[slot, step],
                device_id={"heads": peer}, device_id_type=MESH,
            )
            for slot, peer in ((3, across), (1, right), (2, left))
        ]

    def tile(step, more):
        shift = top[0:1, :]
        total = None
        highest = None
        if more:
            q = make_query(step + 1)
        for start in range(0, LMAX, SPAN):
            place = pl.ds(start, SPAN)
            p = jnp.exp(score[place, :] - shift).astype(BF)
            r = jnp.dot(values[:, place], p, preferred_element_type=F32)
            total = r if total is None else total + r
            if more:
                s = scores(keys[place, :], q, place)
                highest = s if highest is None else jnp.maximum(highest, s)
        if more:
            keep_top(highest)
        ones = total[GROUP : GROUP + 1]
        first = total[:HD, :TILE] / ones[:, :TILE]
        second = total[HD:GROUP, TILE:] / ones[:, TILE:]
        att[0, step] = jnp.concatenate([first, second], axis=0).T.astype(BF)

    def project(step):
        r = jnp.dot(att[0, step], wo_all[0], preferred_element_type=F32)
        for slot in (1, 2, 3):
            r += jnp.dot(att[slot, step], wo_all[slot], preferred_element_type=F32)
        row = step * TILE + lax.broadcasted_iota(jnp.int32, (TILE, GROUP), 0)
        out[0, pl.ds(pl.multiple_of(step * TILE, TILE), TILE), :] = jnp.where(row < count, r, 0.0)

    @pl.loop(0, STEPS - 1)
    def _(step):
        tile(step, True)

        for copy in sends(step):
            copy.start()

    tile(STEPS - 1, False)
    for copy in sends(STEPS - 1):
        copy.start()
    wo_own.wait()
    for copy in wo_sends:
        copy.wait()

    @pl.loop(0, STEPS)
    def _(step):
        for copy in sends(step):
            copy.wait_recv()
        project(step)

    @pl.loop(0, STEPS)
    def _(step):
        for copy in sends(step):
            copy.wait_send()


def body(history, candidates, lengths, counts, w_query, w_key, w_value, w_out):
    in_hbm = pl.BlockSpec(memory_space=pltpu.HBM)
    groups = lax.axis_size("heads")
    return pl.pallas_call(
        kernel,
        out_shape=pltpu.VMEM((1, CMAX, GROUP), F32),
        in_specs=[in_hbm] * 8,
        out_specs=pl.BlockSpec(memory_space=pltpu.VMEM),
        scratch_shapes=[
            pltpu.VMEM((LMAX, D), BF),
            pltpu.VMEM((CMAX, D), BF),
            pltpu.VMEM((D, GROUP), BF),
            pltpu.VMEM((D, 2 * GROUP), BF),
            pltpu.VMEM((GROUP, D), BF),
            pltpu.VMEM((groups, GROUP, GROUP), BF),
            pltpu.VMEM((LMAX, GROUP), BF),
            pltpu.VMEM((VROWS, LMAX), BF),
            pltpu.VMEM((LMAX, WIDE), F32),
            pltpu.VMEM((8, WIDE), F32),
            pltpu.VMEM((groups, STEPS, TILE, GROUP), BF),
            pltpu.SMEM(lengths.shape, jnp.int32),
            pltpu.SMEM(counts.shape, jnp.int32),
            pltpu.SemaphoreType.DMA((8 + len(LOADS),)),
            pltpu.SemaphoreType.DMA((groups,)),
            pltpu.SemaphoreType.DMA((groups,)),
            pltpu.SemaphoreType.DMA((4, STEPS)),
            pltpu.SemaphoreType.DMA((4, STEPS)),
        ],
        compiler_params=pltpu.CompilerParams(
            collective_id=0, has_side_effects=True, vmem_limit_bytes=60 * 2**20
        ),
    )(history, candidates, lengths, counts, w_query, w_key, w_value, w_out)


def solution(mesh):
    placed = (
        P("users", None, None),
        P("users", None, None),
        P(),
        P(),
        P(None, "heads"),
        P(None, "heads"),
        P(None, "heads"),
        P("heads", None),
    )
    return jax.shard_map(
        body, mesh=mesh, in_specs=placed, out_specs=P("users", None, "heads"), check_vma=False
    )
```

```python
import functools

import jax
import jax.numpy as jnp
from jax import lax
from jax.experimental import pallas as pl
from jax.experimental.pallas import tpu as pltpu
from jax.sharding import PartitionSpec as P

D = 512
HD = 64
LMAX = 4096
CMAX = 1024
GROUP = 128
TILE = 128
STEPS = CMAX // TILE
WIDE = 2 * TILE
SPAN = 512
LOAD = 1024
LOADS = LMAX // LOAD
VROWS = GROUP + 16
FOLD = 64
RELAYED = range(2, 7)
LAG = 3
HALF = TILE // 2
MESH = pl.DeviceIdType.MESH
BF = jnp.bfloat16
F32 = jnp.float32


def kernel(
    history, candidates, lengths, counts, w_query, w_key, w_value, w_out, out,
    hist, cand, wq, wkv, wo, wo_all, keys, key0, values, query, best, score, top, att,
    length_of, count_of, load_sem, wo_send, wo_recv, send_sem, recv_sem,
):
    user = lax.axis_index("users")
    me = lax.axis_index("heads")
    ring = lax.axis_size("heads")
    right = lax.rem(me + 1, ring)
    left = lax.rem(me + ring - 1, ring)
    across = lax.rem(me + 2, ring)

    def load(source, target, slot):
        copy = pltpu.make_async_copy(source, target, load_sem.at[slot])
        copy.start()
        return copy

    def load_history(i):
        rows = pl.ds(pl.multiple_of(i * LOAD, LOAD), LOAD)
        return pltpu.make_async_copy(history.at[0, rows], hist.at[rows], load_sem.at[8 + i])

    wk_copy = load(w_key, wkv.at[:, pl.ds(0, GROUP)], 2)
    wv_copy = load(w_value, wkv.at[:, pl.ds(GROUP, GROUP)], 3)
    load_history(0).start()
    length_copy = load(lengths, length_of, 6)
    wq_copy = load(w_query, wq, 0)
    first_cand = load(candidates.at[0, pl.ds(0, TILE)], cand.at[pl.ds(0, TILE)], 1)
    wo_copy = load(w_out, wo, 5)
    for i in range(1, LOADS):
        load_history(i).start()
    count_copy = load(counts, count_of, 7)
    rest_cand = load(
        candidates.at[0, pl.ds(TILE, CMAX - TILE)], cand.at[pl.ds(TILE, CMAX - TILE)], 4
    )

    barrier = pltpu.get_barrier_semaphore()
    for peer in (left, right, across):
        pl.semaphore_signal(barrier, inc=1, device_id={"heads": peer}, device_id_type=MESH)

    def make_query(step):
        rows = cand[pl.ds(pl.multiple_of(step * TILE, TILE), TILE), :]
        q = (jnp.dot(rows, wq[...], preferred_element_type=F32) * HD ** (-0.5)).astype(BF)
        first = lax.broadcasted_iota(jnp.int32, (TILE, GROUP), 1) < HD
        zero = jnp.zeros_like(q)
        return jnp.concatenate([jnp.where(first, q, zero), jnp.where(first, zero, q)], axis=0)

    def scores(k, q, place):
        s = lax.dot_general(k, q, (((1,), (1,)), ((), ())), preferred_element_type=F32)
        score[place, :] = s
        return jnp.max(s.reshape(-1, FOLD, WIDE), axis=0)

    def keep_top(highest):
        top[...] = jnp.broadcast_to(jnp.max(highest, axis=0, keepdims=True), (8, WIDE))

    def block(peer):
        return wo.at[:, pl.ds(pl.multiple_of(peer * GROUP, GROUP), GROUP)]

    wo_own = pltpu.make_async_copy(block(me), wo_all.at[0], wo_send.at[0])
    wo_sends = [
        pltpu.make_async_remote_copy(
            src_ref=block(peer), dst_ref=wo_all.at[slot], send_sem=wo_send.at[slot],
            recv_sem=wo_recv.at[slot], device_id={"heads": peer}, device_id_type=MESH,
        )
        for slot, peer in ((3, across), (1, right), (2, left))
    ]

    def exchange_wo():
        wo_copy.wait()
        pl.semaphore_wait(barrier, 3)
        for copy in wo_sends + [wo_own]:
            copy.start()

    wk_copy.wait()
    wv_copy.wait()
    length_copy.wait()
    length = length_of[user]
    def project_history(i, first):
        for part in range(0, LOAD, 256):
            start = pl.multiple_of(i * LOAD + part, 256)
            place = pl.ds(start, 256)
            kv = jnp.dot(hist[place, :], wkv[...], preferred_element_type=F32)
            if first and part == 0:
                key0[...] = kv[0:8, :GROUP]
            valid = start + lax.broadcasted_iota(jnp.int32, (256, GROUP), 0) < length
            keys[place, :] = jnp.where(valid, kv[:, :GROUP], key0[0:1, :]).astype(BF)
            values[0:GROUP, place] = jnp.where(valid, kv[:, GROUP:], 0.0).T.astype(BF)
            row = lax.broadcasted_iota(jnp.int32, (VROWS - GROUP, 256), 0)
            column = start + lax.broadcasted_iota(jnp.int32, (VROWS - GROUP, 256), 1)
            ones = jnp.where((row == 0) & (column < length), 1.0, 0.0)
            values[GROUP:, place] = ones.astype(BF)

    def first_scores(i):
        highest = None
        for part in range(0, LOAD, 256):
            place = pl.ds(pl.multiple_of(i * LOAD + part, 256), 256)
            s = scores(keys[place, :], query[...], place)
            highest = s if highest is None else jnp.maximum(highest, s)
        return highest

    load_history(0).wait()
    project_history(0, True)
    wq_copy.wait()
    first_cand.wait()
    query[...] = make_query(0)
    best[...] = jnp.full_like(best, -jnp.inf)

    @pl.loop(1, LOADS)
    def _(i):
        pl.when(i == LOADS - 1)(exchange_wo)
        load_history(i).wait()
        best[...] = jnp.maximum(best[...], first_scores(i - 1))
        project_history(i, False)

    keep_top(jnp.maximum(best[...], first_scores(LOADS - 1)))
    rest_cand.wait()
    count_copy.wait()
    count = count_of[user]

    def remote(step, source, slot, sem, peer, rows):
        return pltpu.make_async_remote_copy(
            src_ref=att.at[source, step, rows], dst_ref=att.at[slot, step, rows],
            send_sem=send_sem.at[sem, step], recv_sem=recv_sem.at[sem, step],
            device_id={"heads": peer}, device_id_type=MESH,
        )

    def near(step):
        whole = pl.ds(0, TILE)
        return [remote(step, 0, 1, 1, right, whole), remote(step, 0, 2, 2, left, whole)]

    def far(step):
        return [remote(step, 0, 3, 3, across, pl.ds(0, TILE))]

    def relays(step):
        upper, lower = pl.ds(0, HALF), pl.ds(HALF, HALF)
        return [remote(step, 1, 3, 3, right, upper), remote(step, 2, 3, 0, left, lower)]

    through = lax.rem(user, 2) == 1

    def start(copies):
        for copy in copies:
            copy.start()

    def relay(step):
        for copy in near(step):
            copy.wait_recv()
        start(relays(step))

    def send(step):
        @pl.when((step < RELAYED.start) | (step >= RELAYED.stop) | jnp.logical_not(through))
        def _():
            start(far(step))

        start(near(step))

        @pl.when((step >= LAG + RELAYED.start) & (step < LAG + RELAYED.stop) & through)
        def _():
            relay(step - LAG)

    def tile(step, more):
        shift = top[0:1, :]
        total = None
        highest = None
        if more:
            q = make_query(step + 1)
        for start in range(0, LMAX, SPAN):
            place = pl.ds(start, SPAN)
            p = jnp.exp(score[place, :] - shift).astype(BF)
            r = jnp.dot(values[:, place], p, preferred_element_type=F32)
            total = r if total is None else total + r
            if more:
                s = scores(keys[place, :], q, place)
                highest = s if highest is None else jnp.maximum(highest, s)
        if more:
            keep_top(highest)
        ones = total[GROUP : GROUP + 1]
        first = total[:HD, :TILE] / ones[:, :TILE]
        second = total[HD:GROUP, TILE:] / ones[:, TILE:]
        att[0, step] = jnp.concatenate([first, second], axis=0).T.astype(BF)

    def project(step):
        rows = jnp.concatenate([att[slot, step] for slot in range(4)], axis=1)
        r = jnp.dot(rows, wo_all[...].reshape(4 * GROUP, GROUP), preferred_element_type=F32)
        row = step * TILE + lax.broadcasted_iota(jnp.int32, (TILE, GROUP), 0)
        out[0, pl.ds(pl.multiple_of(step * TILE, TILE), TILE), :] = jnp.where(row < count, r, 0.0)

    @pl.loop(0, STEPS - 1)
    def _(step):
        tile(step, True)
        send(step)

    tile(STEPS - 1, False)
    send(STEPS - 1)
    wo_own.wait()
    for copy in wo_sends:
        copy.wait()
    late = range(STEPS - LAG, RELAYED.stop)
    for step in late:
        pl.when(through)(functools.partial(relay, step))
    for step in range(STEPS):
        if step in RELAYED:
            for copy in near(step):
                copy.wait_send()

            @pl.when(through)
            def _():
                for copy in relays(step):
                    copy.wait()

            @pl.when(jnp.logical_not(through))
            def _():
                for copy in near(step):
                    copy.wait_recv()
                for copy in far(step):
                    copy.wait()

        else:
            for copy in far(step) + near(step):
                copy.wait()
        project(step)


def body(history, candidates, lengths, counts, w_query, w_key, w_value, w_out):
    in_hbm = pl.BlockSpec(memory_space=pltpu.HBM)
    groups = lax.axis_size("heads")
    return pl.pallas_call(
        kernel,
        out_shape=pltpu.VMEM((1, CMAX, GROUP), F32),
        in_specs=[in_hbm] * 8,
        out_specs=pl.BlockSpec(memory_space=pltpu.VMEM),
        scratch_shapes=[
            pltpu.VMEM((LMAX, D), BF),
            pltpu.VMEM((CMAX, D), BF),
            pltpu.VMEM((D, GROUP), BF),
            pltpu.VMEM((D, 2 * GROUP), BF),
            pltpu.VMEM((GROUP, D), BF),
            pltpu.VMEM((groups, GROUP, GROUP), BF),
            pltpu.VMEM((LMAX, GROUP), BF),
            pltpu.VMEM((8, GROUP), F32),
            pltpu.VMEM((VROWS, LMAX), BF),
            pltpu.VMEM((WIDE, GROUP), BF),
            pltpu.VMEM((FOLD, WIDE), F32),
            pltpu.VMEM((LMAX, WIDE), F32),
            pltpu.VMEM((8, WIDE), F32),
            pltpu.VMEM((groups, STEPS, TILE, GROUP), BF),
            pltpu.SMEM(lengths.shape, jnp.int32),
            pltpu.SMEM(counts.shape, jnp.int32),
            pltpu.SemaphoreType.DMA((8 + LOADS,)),
            pltpu.SemaphoreType.DMA((groups,)),
            pltpu.SemaphoreType.DMA((groups,)),
            pltpu.SemaphoreType.DMA((4, STEPS)),
            pltpu.SemaphoreType.DMA((4, STEPS)),
        ],
        compiler_params=pltpu.CompilerParams(
            collective_id=0, has_side_effects=True, vmem_limit_bytes=60 * 2**20
        ),
    )(history, candidates, lengths, counts, w_query, w_key, w_value, w_out)


def solution(mesh):
    placed = (
        P("users", None, None),
        P("users", None, None),
        P(),
        P(),
        P(None, "heads"),
        P(None, "heads"),
        P(None, "heads"),
        P("heads", None),
    )
    return jax.shard_map(
        body, mesh=mesh, in_specs=placed, out_specs=P("users", None, "heads"), check_vma=False
    )
```

```python
import functools

import jax
import jax.numpy as jnp
from jax import lax
from jax.experimental import pallas as pl
from jax.experimental.pallas import tpu as pltpu
from jax.sharding import PartitionSpec as P

D = 512
HD = 64
LMAX = 4096
CMAX = 1024
GROUP = 128
TILE = 128
STEPS = CMAX // TILE
WIDE = 2 * TILE
SPAN = 512
LOADS = (1024, 1024, 2048)
STARTS = tuple(sum(LOADS[:i]) for i in range(len(LOADS)))
VROWS = GROUP + 16
FOLD = 64
RELAYED = range(2, 7)
LAG = 3
HALF = TILE // 2
MESH = pl.DeviceIdType.MESH
BF = jnp.bfloat16
F32 = jnp.float32


def kernel(
    history, candidates, lengths, counts, w_query, w_key, w_value, w_out, out,
    hist, cand, wq, wkv, wo, wo_all, keys, key0, values, query, score, top, att,
    length_of, count_of, load_sem, wo_send, wo_recv, send_sem, recv_sem,
):
    user = lax.axis_index("users")
    me = lax.axis_index("heads")
    ring = lax.axis_size("heads")
    right = lax.rem(me + 1, ring)
    left = lax.rem(me + ring - 1, ring)
    across = lax.rem(me + 2, ring)

    def load(source, target, slot):
        copy = pltpu.make_async_copy(source, target, load_sem.at[slot])
        copy.start()
        return copy

    def load_history(i):
        rows = pl.ds(STARTS[i], LOADS[i])
        return pltpu.make_async_copy(history.at[0, rows], hist.at[rows], load_sem.at[8 + i])

    wk_copy = load(w_key, wkv.at[:, pl.ds(0, GROUP)], 2)
    wv_copy = load(w_value, wkv.at[:, pl.ds(GROUP, GROUP)], 3)
    load_history(0).start()
    length_copy = load(lengths, length_of, 6)
    wq_copy = load(w_query, wq, 0)
    first_cand = load(candidates.at[0, pl.ds(0, TILE)], cand.at[pl.ds(0, TILE)], 1)
    wo_copy = load(w_out, wo, 5)
    for i in range(1, len(LOADS)):
        load_history(i).start()
    count_copy = load(counts, count_of, 7)
    rest_cand = load(
        candidates.at[0, pl.ds(TILE, CMAX - TILE)], cand.at[pl.ds(TILE, CMAX - TILE)], 4
    )

    barrier = pltpu.get_barrier_semaphore()
    for peer in (left, right, across):
        pl.semaphore_signal(barrier, inc=1, device_id={"heads": peer}, device_id_type=MESH)

    def make_query(step):
        rows = cand[pl.ds(pl.multiple_of(step * TILE, TILE), TILE), :]
        q = (jnp.dot(rows, wq[...], preferred_element_type=F32) * HD ** (-0.5)).astype(BF)
        first = lax.broadcasted_iota(jnp.int32, (TILE, GROUP), 1) < HD
        zero = jnp.zeros_like(q)
        return jnp.concatenate([jnp.where(first, q, zero), jnp.where(first, zero, q)], axis=0)

    def scores(k, q, place):
        s = lax.dot_general(k, q, (((1,), (1,)), ((), ())), preferred_element_type=F32)
        score[place, :] = s
        return jnp.max(s.reshape(-1, FOLD, WIDE), axis=0)

    def keep_top(highest):
        top[...] = jnp.broadcast_to(jnp.max(highest, axis=0, keepdims=True), (8, WIDE))

    def block(peer):
        return wo.at[:, pl.ds(pl.multiple_of(peer * GROUP, GROUP), GROUP)]

    wo_own = pltpu.make_async_copy(block(me), wo_all.at[0], wo_send.at[0])
    wo_sends = [
        pltpu.make_async_remote_copy(
            src_ref=block(peer), dst_ref=wo_all.at[slot], send_sem=wo_send.at[slot],
            recv_sem=wo_recv.at[slot], device_id={"heads": peer}, device_id_type=MESH,
        )
        for slot, peer in ((3, across), (1, right), (2, left))
    ]

    def exchange_wo():
        wo_copy.wait()
        pl.semaphore_wait(barrier, 3)
        for copy in wo_sends + [wo_own]:
            copy.start()

    wk_copy.wait()
    wv_copy.wait()
    length_copy.wait()
    length = length_of[user]
    def project_history(i):
        for start in range(STARTS[i], STARTS[i] + LOADS[i], 256):
            place = pl.ds(start, 256)
            kv = jnp.dot(hist[place, :], wkv[...], preferred_element_type=F32)
            if start == 0:
                key0[...] = kv[0:8, :GROUP]
            valid = start + lax.broadcasted_iota(jnp.int32, (256, GROUP), 0) < length
            keys[place, :] = jnp.where(valid, kv[:, :GROUP], key0[0:1, :]).astype(BF)
            values[0:GROUP, place] = jnp.where(valid, kv[:, GROUP:], 0.0).T.astype(BF)
            row = lax.broadcasted_iota(jnp.int32, (VROWS - GROUP, 256), 0)
            column = start + lax.broadcasted_iota(jnp.int32, (VROWS - GROUP, 256), 1)
            ones = jnp.where((row == 0) & (column < length), 1.0, 0.0)
            values[GROUP:, place] = ones.astype(BF)

    def first_scores(i):
        highest = None
        for start in range(STARTS[i], STARTS[i] + LOADS[i], 256):
            place = pl.ds(start, 256)
            s = scores(keys[place, :], q, place)
            highest = s if highest is None else jnp.maximum(highest, s)
        return highest

    load_history(0).wait()
    project_history(0)
    wq_copy.wait()
    first_cand.wait()
    q = make_query(0)
    highest = None
    for i in range(1, len(LOADS)):
        if i == 2:
            exchange_wo()
        load_history(i).wait()
        s = first_scores(i - 1)
        highest = s if highest is None else jnp.maximum(highest, s)
        project_history(i)
    keep_top(jnp.maximum(highest, first_scores(len(LOADS) - 1)))
    rest_cand.wait()
    query[...] = make_query(1)
    count_copy.wait()
    count = count_of[user]

    def remote(step, source, slot, sem, peer, rows):
        return pltpu.make_async_remote_copy(
            src_ref=att.at[source, step, rows], dst_ref=att.at[slot, step, rows],
            send_sem=send_sem.at[sem, step], recv_sem=recv_sem.at[sem, step],
            device_id={"heads": peer}, device_id_type=MESH,
        )

    def near(step):
        whole = pl.ds(0, TILE)
        return [remote(step, 0, 1, 1, right, whole), remote(step, 0, 2, 2, left, whole)]

    def far(step):
        return [remote(step, 0, 3, 3, across, pl.ds(0, TILE))]

    def relays(step):
        upper, lower = pl.ds(0, HALF), pl.ds(HALF, HALF)
        return [remote(step, 1, 3, 3, right, upper), remote(step, 2, 3, 0, left, lower)]

    through = lax.rem(user, 2) == 1

    def start(copies):
        for copy in copies:
            copy.start()

    def relay(step):
        for copy in near(step):
            copy.wait_recv()
        start(relays(step))

    def send(step):
        @pl.when((step < RELAYED.start) | (step >= RELAYED.stop) | jnp.logical_not(through))
        def _():
            start(far(step))

        start(near(step))

        @pl.when((step >= LAG + RELAYED.start) & (step < LAG + RELAYED.stop) & through)
        def _():
            relay(step - LAG)

    def tile(step, more):
        shift = top[0:1, :]
        total = None
        highest = None
        if more:
            q = query[...]
            query[...] = make_query(lax.rem(step + 2, STEPS))
        for start in range(0, LMAX, SPAN):
            place = pl.ds(start, SPAN)
            p = jnp.exp(score[place, :] - shift).astype(BF)
            r = jnp.dot(values[:, place], p, preferred_element_type=F32)
            total = r if total is None else total + r
            if more:
                size = SPAN // 2
                for part in range(start, start + SPAN, size):
                    place = pl.ds(part, size)
                    s = scores(keys[place, :], q, place)
                    highest = s if highest is None else jnp.maximum(highest, s)
        if more:
            keep_top(highest)
        ones = total[GROUP : GROUP + 1]
        first = total[:HD, :TILE] / ones[:, :TILE]
        second = total[HD:GROUP, TILE:] / ones[:, TILE:]
        att[0, step] = jnp.concatenate([first, second], axis=0).T.astype(BF)

    def project(step):
        rows = jnp.concatenate([att[slot, step] for slot in range(4)], axis=1)
        r = jnp.dot(rows, wo_all[...].reshape(4 * GROUP, GROUP), preferred_element_type=F32)
        row = step * TILE + lax.broadcasted_iota(jnp.int32, (TILE, GROUP), 0)
        out[0, pl.ds(pl.multiple_of(step * TILE, TILE), TILE), :] = jnp.where(row < count, r, 0.0)

    @pl.loop(0, STEPS - 1)
    def _(step):
        tile(step, True)
        send(step)

    tile(STEPS - 1, False)
    send(STEPS - 1)
    wo_own.wait()
    for copy in wo_sends:
        copy.wait()
    late = range(STEPS - LAG, RELAYED.stop)
    for step in late:
        pl.when(through)(functools.partial(relay, step))
    for step in range(STEPS):
        if step in RELAYED:
            for copy in near(step):
                copy.wait_send()

            @pl.when(through)
            def _():
                for copy in relays(step):
                    copy.wait()

            @pl.when(jnp.logical_not(through))
            def _():
                for copy in near(step):
                    copy.wait_recv()
                for copy in far(step):
                    copy.wait()

        else:
            for copy in far(step) + near(step):
                copy.wait()
        project(step)


def body(history, candidates, lengths, counts, w_query, w_key, w_value, w_out):
    in_hbm = pl.BlockSpec(memory_space=pltpu.HBM)
    groups = lax.axis_size("heads")
    return pl.pallas_call(
        kernel,
        out_shape=pltpu.VMEM((1, CMAX, GROUP), F32),
        in_specs=[in_hbm] * 8,
        out_specs=pl.BlockSpec(memory_space=pltpu.VMEM),
        scratch_shapes=[
            pltpu.VMEM((LMAX, D), BF),
            pltpu.VMEM((CMAX, D), BF),
            pltpu.VMEM((D, GROUP), BF),
            pltpu.VMEM((D, 2 * GROUP), BF),
            pltpu.VMEM((GROUP, D), BF),
            pltpu.VMEM((groups, GROUP, GROUP), BF),
            pltpu.VMEM((LMAX, GROUP), BF),
            pltpu.VMEM((8, GROUP), F32),
            pltpu.VMEM((VROWS, LMAX), BF),
            pltpu.VMEM((WIDE, GROUP), BF),
            pltpu.VMEM((LMAX, WIDE), F32),
            pltpu.VMEM((8, WIDE), F32),
            pltpu.VMEM((groups, STEPS, TILE, GROUP), BF),
            pltpu.SMEM(lengths.shape, jnp.int32),
            pltpu.SMEM(counts.shape, jnp.int32),
            pltpu.SemaphoreType.DMA((8 + len(LOADS),)),
            pltpu.SemaphoreType.DMA((groups,)),
            pltpu.SemaphoreType.DMA((groups,)),
            pltpu.SemaphoreType.DMA((4, STEPS)),
            pltpu.SemaphoreType.DMA((4, STEPS)),
        ],
        compiler_params=pltpu.CompilerParams(
            collective_id=0, has_side_effects=True, vmem_limit_bytes=60 * 2**20
        ),
    )(history, candidates, lengths, counts, w_query, w_key, w_value, w_out)


def solution(mesh):
    placed = (
        P("users", None, None),
        P("users", None, None),
        P(),
        P(),
        P(None, "heads"),
        P(None, "heads"),
        P(None, "heads"),
        P("heads", None),
    )
    return jax.shard_map(
        body, mesh=mesh, in_specs=placed, out_specs=P("users", None, "heads"), check_vma=False
    )
```

```python
import functools

import jax
import jax.numpy as jnp
from jax import lax
from jax.experimental import pallas as pl
from jax.experimental.pallas import tpu as pltpu
from jax.sharding import PartitionSpec as P

D = 512
HD = 64
LMAX = 4096
CMAX = 1024
GROUP = 128
TILE = 128
STEPS = CMAX // TILE
WIDE = 2 * TILE
SPAN = 512
LOADS = (1024, 1024, 2048)
STARTS = tuple(sum(LOADS[:i]) for i in range(len(LOADS)))
VROWS = GROUP + 16
FOLD = 64
RELAYED = range(2, 7)
LAG = 4
HALF = TILE // 2
MESH = pl.DeviceIdType.MESH
BF = jnp.bfloat16
F32 = jnp.float32


def kernel(
    history, candidates, lengths, counts, w_query, w_key, w_value, w_out, out,
    hist, cand, wq, wkv, wo, wo_all, keys, key0, values, query, score, top, att,
    length_of, count_of, load_sem, wo_send, wo_recv, send_sem, recv_sem,
):
    user = lax.axis_index("users")
    me = lax.axis_index("heads")
    ring = lax.axis_size("heads")
    right = lax.rem(me + 1, ring)
    left = lax.rem(me + ring - 1, ring)
    across = lax.rem(me + 2, ring)

    def load(source, target, slot):
        copy = pltpu.make_async_copy(source, target, load_sem.at[slot])
        copy.start()
        return copy

    def load_history(i):
        rows = pl.ds(STARTS[i], LOADS[i])
        return pltpu.make_async_copy(history.at[0, rows], hist.at[rows], load_sem.at[8 + i])

    wk_copy = load(w_key, wkv.at[:, pl.ds(0, GROUP)], 2)
    wv_copy = load(w_value, wkv.at[:, pl.ds(GROUP, GROUP)], 3)
    load_history(0).start()
    length_copy = load(lengths, length_of, 6)
    wq_copy = load(w_query, wq, 0)
    first_cand = load(candidates.at[0, pl.ds(0, TILE)], cand.at[pl.ds(0, TILE)], 1)
    wo_copy = load(w_out, wo, 5)
    for i in range(1, len(LOADS)):
        load_history(i).start()
    count_copy = load(counts, count_of, 7)
    rest_cand = load(
        candidates.at[0, pl.ds(TILE, CMAX - TILE)], cand.at[pl.ds(TILE, CMAX - TILE)], 4
    )

    barrier = pltpu.get_barrier_semaphore()
    for peer in (left, right, across):
        pl.semaphore_signal(barrier, inc=1, device_id={"heads": peer}, device_id_type=MESH)

    def make_query(step):
        rows = cand[pl.ds(pl.multiple_of(step * TILE, TILE), TILE), :]
        q = (jnp.dot(rows, wq[...], preferred_element_type=F32) * HD ** (-0.5)).astype(BF)
        first = lax.broadcasted_iota(jnp.int32, (TILE, GROUP), 1) < HD
        zero = jnp.zeros_like(q)
        return jnp.concatenate([jnp.where(first, q, zero), jnp.where(first, zero, q)], axis=0)

    def scores(k, q, place):
        s = lax.dot_general(k, q, (((1,), (1,)), ((), ())), preferred_element_type=F32)
        score[place, :] = s
        return jnp.max(s.reshape(-1, FOLD, WIDE), axis=0)

    def keep_top(highest):
        top[...] = jnp.broadcast_to(jnp.max(highest, axis=0, keepdims=True), (8, WIDE))

    def block(peer):
        return wo.at[:, pl.ds(pl.multiple_of(peer * GROUP, GROUP), GROUP)]

    wo_own = pltpu.make_async_copy(block(me), wo_all.at[0], wo_send.at[0])
    wo_sends = [
        pltpu.make_async_remote_copy(
            src_ref=block(peer), dst_ref=wo_all.at[slot], send_sem=wo_send.at[slot],
            recv_sem=wo_recv.at[slot], device_id={"heads": peer}, device_id_type=MESH,
        )
        for slot, peer in ((3, across), (1, right), (2, left))
    ]

    def exchange_wo():
        wo_copy.wait()
        pl.semaphore_wait(barrier, 3)
        for copy in wo_sends + [wo_own]:
            copy.start()

    wk_copy.wait()
    wv_copy.wait()
    length_copy.wait()
    length = length_of[user]
    def project_history(i):
        for start in range(STARTS[i], STARTS[i] + LOADS[i], 256):
            place = pl.ds(start, 256)
            kv = jnp.dot(hist[place, :], wkv[...], preferred_element_type=F32)
            if start == 0:
                key0[...] = kv[0:8, :GROUP]
            valid = start + lax.broadcasted_iota(jnp.int32, (256, GROUP), 0) < length
            keys[place, :] = jnp.where(valid, kv[:, :GROUP], key0[0:1, :]).astype(BF)
            values[0:GROUP, place] = jnp.where(valid, kv[:, GROUP:], 0.0).T.astype(BF)
            row = lax.broadcasted_iota(jnp.int32, (VROWS - GROUP, 256), 0)
            column = start + lax.broadcasted_iota(jnp.int32, (VROWS - GROUP, 256), 1)
            ones = jnp.where((row == 0) & (column < length), 1.0, 0.0)
            values[GROUP:, place] = ones.astype(BF)

    def first_scores(i):
        highest = None
        for start in range(STARTS[i], STARTS[i] + LOADS[i], 256):
            place = pl.ds(start, 256)
            s = scores(keys[place, :], q, place)
            highest = s if highest is None else jnp.maximum(highest, s)
        return highest

    load_history(0).wait()
    project_history(0)
    wq_copy.wait()
    first_cand.wait()
    q = make_query(0)
    highest = None
    for i in range(1, len(LOADS)):
        if i == 2:
            exchange_wo()
        load_history(i).wait()
        s = first_scores(i - 1)
        highest = s if highest is None else jnp.maximum(highest, s)
        project_history(i)
    keep_top(jnp.maximum(highest, first_scores(len(LOADS) - 1)))
    rest_cand.wait()
    query[...] = make_query(1)
    count_copy.wait()
    count = count_of[user]

    def remote(step, source, slot, sem, peer, rows):
        return pltpu.make_async_remote_copy(
            src_ref=att.at[source, step, rows], dst_ref=att.at[slot, step, rows],
            send_sem=send_sem.at[sem, step], recv_sem=recv_sem.at[sem, step],
            device_id={"heads": peer}, device_id_type=MESH,
        )

    def near(step):
        whole = pl.ds(0, TILE)
        return [remote(step, 0, 1, 1, right, whole), remote(step, 0, 2, 2, left, whole)]

    def far(step):
        return [remote(step, 0, 3, 3, across, pl.ds(0, TILE))]

    def relays(step):
        upper, lower = pl.ds(0, HALF), pl.ds(HALF, HALF)
        return [remote(step, 1, 3, 3, right, upper), remote(step, 2, 3, 0, left, lower)]

    through = lax.rem(user, 2) == 1

    def start(copies):
        for copy in copies:
            copy.start()

    def relay(step):
        for copy in near(step):
            copy.wait_recv()
        start(relays(step))

    def send(step):
        @pl.when((step < RELAYED.start) | (step >= RELAYED.stop) | jnp.logical_not(through))
        def _():
            start(far(step))

        start(near(step))

        @pl.when((step >= LAG + RELAYED.start) & (step < LAG + RELAYED.stop) & through)
        def _():
            relay(step - LAG)

    def tile(step, more):
        shift = top[0:1, :]
        total = None
        highest = None
        if more:
            q = query[...]
            query[...] = make_query(lax.rem(step + 2, STEPS))
        for start in range(0, LMAX, SPAN):
            place = pl.ds(start, SPAN)
            p = jnp.exp(score[place, :] - shift).astype(BF)
            r = jnp.dot(values[:, place], p, preferred_element_type=F32)
            total = r if total is None else total + r
            if more:
                size = SPAN // 2
                for part in range(start, start + SPAN, size):
                    place = pl.ds(part, size)
                    s = scores(keys[place, :], q, place)
                    highest = s if highest is None else jnp.maximum(highest, s)
        if more:
            keep_top(highest)
        ones = total[GROUP : GROUP + 1]
        first = total[:HD, :TILE] / ones[:, :TILE]
        second = total[HD:GROUP, TILE:] / ones[:, TILE:]
        att[0, step] = jnp.concatenate([first, second], axis=0).T.astype(BF)

    def project(step):
        rows = jnp.concatenate([att[slot, step] for slot in range(4)], axis=1)
        r = jnp.dot(rows, wo_all[...].reshape(4 * GROUP, GROUP), preferred_element_type=F32)
        row = step * TILE + lax.broadcasted_iota(jnp.int32, (TILE, GROUP), 0)
        out[0, pl.ds(pl.multiple_of(step * TILE, TILE), TILE), :] = jnp.where(row < count, r, 0.0)

    @pl.loop(0, STEPS - 1)
    def _(step):
        tile(step, True)
        send(step)

    tile(STEPS - 1, False)
    send(STEPS - 1)
    wo_own.wait()
    for copy in wo_sends:
        copy.wait()
    late = range(STEPS - LAG, RELAYED.stop)
    for step in late:
        pl.when(through)(functools.partial(relay, step))
    for step in range(STEPS):
        if step in RELAYED:
            for copy in near(step):
                copy.wait_send()

            @pl.when(through)
            def _():
                for copy in relays(step):
                    copy.wait()

            @pl.when(jnp.logical_not(through))
            def _():
                for copy in near(step):
                    copy.wait_recv()
                for copy in far(step):
                    copy.wait()

        else:
            for copy in far(step) + near(step):
                copy.wait()
        project(step)


def body(history, candidates, lengths, counts, w_query, w_key, w_value, w_out):
    in_hbm = pl.BlockSpec(memory_space=pltpu.HBM)
    groups = lax.axis_size("heads")
    return pl.pallas_call(
        kernel,
        out_shape=pltpu.VMEM((1, CMAX, GROUP), F32),
        in_specs=[in_hbm] * 8,
        out_specs=pl.BlockSpec(memory_space=pltpu.VMEM),
        scratch_shapes=[
            pltpu.VMEM((LMAX, D), BF),
            pltpu.VMEM((CMAX, D), BF),
            pltpu.VMEM((D, GROUP), BF),
            pltpu.VMEM((D, 2 * GROUP), BF),
            pltpu.VMEM((GROUP, D), BF),
            pltpu.VMEM((groups, GROUP, GROUP), BF),
            pltpu.VMEM((LMAX, GROUP), BF),
            pltpu.VMEM((8, GROUP), F32),
            pltpu.VMEM((VROWS, LMAX), BF),
            pltpu.VMEM((WIDE, GROUP), BF),
            pltpu.VMEM((LMAX, WIDE), F32),
            pltpu.VMEM((8, WIDE), F32),
            pltpu.VMEM((groups, STEPS, TILE, GROUP), BF),
            pltpu.SMEM(lengths.shape, jnp.int32),
            pltpu.SMEM(counts.shape, jnp.int32),
            pltpu.SemaphoreType.DMA((8 + len(LOADS),)),
            pltpu.SemaphoreType.DMA((groups,)),
            pltpu.SemaphoreType.DMA((groups,)),
            pltpu.SemaphoreType.DMA((4, STEPS)),
            pltpu.SemaphoreType.DMA((4, STEPS)),
        ],
        compiler_params=pltpu.CompilerParams(
            collective_id=0, has_side_effects=True, vmem_limit_bytes=60 * 2**20
        ),
    )(history, candidates, lengths, counts, w_query, w_key, w_value, w_out)


def solution(mesh):
    placed = (
        P("users", None, None),
        P("users", None, None),
        P(),
        P(),
        P(None, "heads"),
        P(None, "heads"),
        P(None, "heads"),
        P("heads", None),
    )
    return jax.shard_map(
        body, mesh=mesh, in_specs=placed, out_specs=P("users", None, "heads"), check_vma=False
    )
```

```python
import functools

import jax
import jax.numpy as jnp
from jax import lax
from jax.experimental import pallas as pl
from jax.experimental.pallas import tpu as pltpu
from jax.sharding import PartitionSpec as P

D = 512
HD = 64
LMAX = 4096
CMAX = 1024
GROUP = 128
TILE = 128
STEPS = CMAX // TILE
WIDE = 2 * TILE
SPAN = 512
LAST_SPAN = 1024
LOADS = (1024, 1024, 2048)
STARTS = tuple(sum(LOADS[:i]) for i in range(len(LOADS)))
VROWS = GROUP + 16
FOLD = 32
RELAYED = range(2, 7)
LAG = 4
HALF = TILE // 2
MESH = pl.DeviceIdType.MESH
BF = jnp.bfloat16
F32 = jnp.float32


def kernel(
    history, candidates, lengths, counts, w_query, w_key, w_value, w_out, out,
    hist, cand, wq, wkv, wo, wo_all, keys, key0, values, query, score, top, att,
    length_of, count_of, load_sem, wo_send, wo_recv, send_sem, recv_sem,
):
    user = lax.axis_index("users")
    me = lax.axis_index("heads")
    ring = lax.axis_size("heads")
    right = lax.rem(me + 1, ring)
    left = lax.rem(me + ring - 1, ring)
    across = lax.rem(me + 2, ring)

    def load(source, target, slot):
        copy = pltpu.make_async_copy(source, target, load_sem.at[slot])
        copy.start()
        return copy

    def load_history(i):
        rows = pl.ds(STARTS[i], LOADS[i])
        return pltpu.make_async_copy(history.at[0, rows], hist.at[rows], load_sem.at[8 + i])

    wk_copy = load(w_key, wkv.at[:, pl.ds(0, GROUP)], 2)
    wv_copy = load(w_value, wkv.at[:, pl.ds(GROUP, GROUP)], 3)
    load_history(0).start()
    length_copy = load(lengths, length_of, 6)
    wq_copy = load(w_query, wq, 0)
    first_cand = load(candidates.at[0, pl.ds(0, TILE)], cand.at[pl.ds(0, TILE)], 1)
    wo_copy = load(w_out, wo, 5)
    for i in range(1, len(LOADS)):
        load_history(i).start()
    count_copy = load(counts, count_of, 7)
    rest_cand = load(
        candidates.at[0, pl.ds(TILE, CMAX - TILE)], cand.at[pl.ds(TILE, CMAX - TILE)], 4
    )

    barrier = pltpu.get_barrier_semaphore()
    for peer in (left, right, across):
        pl.semaphore_signal(barrier, inc=1, device_id={"heads": peer}, device_id_type=MESH)

    def make_query(step):
        rows = cand[pl.ds(pl.multiple_of(step * TILE, TILE), TILE), :]
        q = (jnp.dot(rows, wq[...], preferred_element_type=F32) * HD ** (-0.5)).astype(BF)
        first = lax.broadcasted_iota(jnp.int32, (TILE, GROUP), 1) < HD
        zero = jnp.zeros_like(q)
        return jnp.concatenate([jnp.where(first, q, zero), jnp.where(first, zero, q)], axis=0)

    def scores(k, q, place):
        s = lax.dot_general(k, q, (((1,), (1,)), ((), ())), preferred_element_type=F32)
        score[place, :] = s
        return jnp.max(s.reshape(-1, FOLD, WIDE), axis=0)

    def keep_top(highest):
        top[...] = jnp.broadcast_to(jnp.max(highest, axis=0, keepdims=True), (8, WIDE))

    def block(peer):
        return wo.at[:, pl.ds(pl.multiple_of(peer * GROUP, GROUP), GROUP)]

    wo_own = pltpu.make_async_copy(block(me), wo_all.at[0], wo_send.at[0])
    wo_sends = [
        pltpu.make_async_remote_copy(
            src_ref=block(peer), dst_ref=wo_all.at[slot], send_sem=wo_send.at[slot],
            recv_sem=wo_recv.at[slot], device_id={"heads": peer}, device_id_type=MESH,
        )
        for slot, peer in ((3, across), (1, right), (2, left))
    ]

    def exchange_wo():
        wo_copy.wait()
        pl.semaphore_wait(barrier, 3)
        for copy in wo_sends + [wo_own]:
            copy.start()

    wk_copy.wait()
    wv_copy.wait()
    length_copy.wait()
    length = length_of[user]
    def project_history(i):
        for start in range(STARTS[i], STARTS[i] + LOADS[i], 256):
            place = pl.ds(start, 256)
            kv = jnp.dot(hist[place, :], wkv[...], preferred_element_type=F32)
            if start == 0:
                key0[...] = kv[0:8, :GROUP]
            valid = start + lax.broadcasted_iota(jnp.int32, (256, GROUP), 0) < length
            keys[place, :] = jnp.where(valid, kv[:, :GROUP], key0[0:1, :]).astype(BF)
            values[0:GROUP, place] = jnp.where(valid, kv[:, GROUP:], 0.0).T.astype(BF)
            row = lax.broadcasted_iota(jnp.int32, (VROWS - GROUP, 256), 0)
            column = start + lax.broadcasted_iota(jnp.int32, (VROWS - GROUP, 256), 1)
            ones = jnp.where((row == 0) & (column < length), 1.0, 0.0)
            values[GROUP:, place] = ones.astype(BF)

    def first_scores(i):
        highest = None
        for start in range(STARTS[i], STARTS[i] + LOADS[i], 256):
            place = pl.ds(start, 256)
            s = scores(keys[place, :], q, place)
            highest = s if highest is None else jnp.maximum(highest, s)
        return highest

    load_history(0).wait()
    project_history(0)
    wq_copy.wait()
    first_cand.wait()
    q = make_query(0)
    highest = None
    for i in range(1, len(LOADS)):
        if i == 2:
            exchange_wo()
        load_history(i).wait()
        s = first_scores(i - 1)
        highest = s if highest is None else jnp.maximum(highest, s)
        project_history(i)
    keep_top(jnp.maximum(highest, first_scores(len(LOADS) - 1)))
    rest_cand.wait()
    query[...] = make_query(1)
    count_copy.wait()
    count = count_of[user]

    def remote(step, source, slot, sem, peer, rows):
        return pltpu.make_async_remote_copy(
            src_ref=att.at[source, step, rows], dst_ref=att.at[slot, step, rows],
            send_sem=send_sem.at[sem, step], recv_sem=recv_sem.at[sem, step],
            device_id={"heads": peer}, device_id_type=MESH,
        )

    def near(step):
        whole = pl.ds(0, TILE)
        return [remote(step, 0, 1, 1, right, whole), remote(step, 0, 2, 2, left, whole)]

    def far(step):
        return [remote(step, 0, 3, 3, across, pl.ds(0, TILE))]

    def relays(step):
        upper, lower = pl.ds(0, HALF), pl.ds(HALF, HALF)
        return [remote(step, 1, 3, 3, right, upper), remote(step, 2, 3, 0, left, lower)]

    through = lax.rem(user, 2) == 1

    def start(copies):
        for copy in copies:
            copy.start()

    def relay(step):
        for copy in near(step):
            copy.wait_recv()
        start(relays(step))

    def send(step):
        @pl.when((step < RELAYED.start) | (step >= RELAYED.stop) | jnp.logical_not(through))
        def _():
            start(far(step))

        start(near(step))

        @pl.when((step >= LAG + RELAYED.start) & (step < LAG + RELAYED.stop) & through)
        def _():
            relay(step - LAG)

    def tile(step, more):
        shift = top[0:1, :]
        total = None
        highest = None
        if more:
            q = query[...]
            query[...] = make_query(lax.rem(step + 2, STEPS))
        span = SPAN if more else LAST_SPAN
        for start in range(0, LMAX, span):
            place = pl.ds(start, span)
            p = jnp.exp(score[place, :] - shift).astype(BF)
            r = jnp.dot(values[:, place], p, preferred_element_type=F32)
            total = r if total is None else total + r
            if more:
                size = SPAN // 2
                for part in range(start, start + SPAN, size):
                    place = pl.ds(part, size)
                    s = scores(keys[place, :], q, place)
                    highest = s if highest is None else jnp.maximum(highest, s)
        if more:
            keep_top(highest)
        ones = total[GROUP : GROUP + 1]
        first = total[:HD, :TILE] / ones[:, :TILE]
        second = total[HD:GROUP, TILE:] / ones[:, TILE:]
        att[0, step] = jnp.concatenate([first, second], axis=0).T.astype(BF)

    def project(step):
        rows = jnp.concatenate([att[slot, step] for slot in range(4)], axis=1)
        r = jnp.dot(rows, wo_all[...].reshape(4 * GROUP, GROUP), preferred_element_type=F32)
        row = step * TILE + lax.broadcasted_iota(jnp.int32, (TILE, GROUP), 0)
        out[0, pl.ds(pl.multiple_of(step * TILE, TILE), TILE), :] = jnp.where(row < count, r, 0.0)

    @pl.loop(0, STEPS - 1)
    def _(step):
        tile(step, True)
        send(step)

    tile(STEPS - 1, False)
    send(STEPS - 1)
    wo_own.wait()
    for copy in wo_sends:
        copy.wait()
    late = range(STEPS - LAG, RELAYED.stop)
    for step in late:
        pl.when(through)(functools.partial(relay, step))
    for step in range(STEPS):
        if step in RELAYED:
            for copy in near(step):
                copy.wait_send()

            @pl.when(through)
            def _():
                for copy in relays(step):
                    copy.wait()

            @pl.when(jnp.logical_not(through))
            def _():
                for copy in near(step):
                    copy.wait_recv()
                for copy in far(step):
                    copy.wait()

        else:
            for copy in far(step) + near(step):
                copy.wait()
        project(step)


def body(history, candidates, lengths, counts, w_query, w_key, w_value, w_out):
    in_hbm = pl.BlockSpec(memory_space=pltpu.HBM)
    groups = lax.axis_size("heads")
    return pl.pallas_call(
        kernel,
        out_shape=pltpu.VMEM((1, CMAX, GROUP), F32),
        in_specs=[in_hbm] * 8,
        out_specs=pl.BlockSpec(memory_space=pltpu.VMEM),
        scratch_shapes=[
            pltpu.VMEM((LMAX, D), BF),
            pltpu.VMEM((CMAX, D), BF),
            pltpu.VMEM((D, GROUP), BF),
            pltpu.VMEM((D, 2 * GROUP), BF),
            pltpu.VMEM((GROUP, D), BF),
            pltpu.VMEM((groups, GROUP, GROUP), BF),
            pltpu.VMEM((LMAX, GROUP), BF),
            pltpu.VMEM((8, GROUP), F32),
            pltpu.VMEM((VROWS, LMAX), BF),
            pltpu.VMEM((WIDE, GROUP), BF),
            pltpu.VMEM((LMAX, WIDE), F32),
            pltpu.VMEM((8, WIDE), F32),
            pltpu.VMEM((groups, STEPS, TILE, GROUP), BF),
            pltpu.SMEM(lengths.shape, jnp.int32),
            pltpu.SMEM(counts.shape, jnp.int32),
            pltpu.SemaphoreType.DMA((8 + len(LOADS),)),
            pltpu.SemaphoreType.DMA((groups,)),
            pltpu.SemaphoreType.DMA((groups,)),
            pltpu.SemaphoreType.DMA((4, STEPS)),
            pltpu.SemaphoreType.DMA((4, STEPS)),
        ],
        compiler_params=pltpu.CompilerParams(
            collective_id=0, has_side_effects=True, vmem_limit_bytes=60 * 2**20
        ),
    )(history, candidates, lengths, counts, w_query, w_key, w_value, w_out)


def solution(mesh):
    placed = (
        P("users", None, None),
        P("users", None, None),
        P(),
        P(),
        P(None, "heads"),
        P(None, "heads"),
        P(None, "heads"),
        P("heads", None),
    )
    return jax.shard_map(
        body, mesh=mesh, in_specs=placed, out_specs=P("users", None, "heads"), check_vma=False
    )
```
